512 devices in a mesh: pt: 64 (over y, z_hi, x), cen: 8 (over z_lo, core).
Axes of the slice: x: 4, y: 4, z: 16 (z_hi: 4, z_lo: 4; z = z_hi * 4 + z_lo), core: 2. Of those that a mesh axis runs over, the one named last changes fastest.
Arguments:
- points: float32 [32768, 1024], P('pt'), may hold values from -6 to 6
- centroids: float32 [2048, 1024], P('cen'), may hold values from -0.03125 to 0.03125
Outputs:
- final_centroids: float32 [8, 256, 1024], P('cen', 'pt')
- log_normaliser: float32 [32768], P('pt')
The draws below stay inside these ranges and needn't reach their ends.
All inputs are finite; a program needn't handle non-finite values.
Results may differ from the reference program's by a relative error of at most 0.0014.
Values sent between devices are 32-bit elements; how exact they have to be, the bound alone decides.
No kernel may reach another device: no remote copies, remote signals or barrier semaphores. Data moves between devices by JAX's collectives and lax.ppermute only.
A program may use at most 64 MiB of HBM per device.

```python
import math
import jax
import jax.numpy as jnp
from jax import lax

D = 1024
K_DEV = 256
ITERS = 2
NPTS = 32768
K = 2048
N_CEN = 8


def signed_rows(key):
    flips = jax.random.bernoulli(key, 0.5, (K, D))
    return jnp.where(flips, 1.0, -1.0).astype(jnp.float32) / jnp.sqrt(jnp.float32(D))


def draw_centroids(key, part):
    shared = signed_rows(key)
    return shared


def draw_points(key, part):
    key = jax.random.fold_in(key, 2)
    key_base, key_scale = jax.random.split(key, 2)
    scales = 0.1 * jnp.exp(jax.random.uniform(key_scale, (NPTS, 1)) * jnp.log(10.0))
    values = jax.random.normal(key_base, (NPTS, D)) * scales
    return jnp.clip(values, -6.0, 6.0).astype(jnp.float32)


def setup_inputs(seed: int = 0) -> dict:
    key_of = jax.random.split(jax.random.key(seed), 3)
    return {
        "points": draw_points(jax.random.fold_in(key_of[2], 71), 0),
        "centroids": draw_centroids(jax.random.fold_in(key_of[2], 71), 0),
    }


tau = 0.1

def one_iteration(points, cent):
    block = math.gcd(NPTS, 4096)
    blocks = points.reshape(NPTS // block, block, D)

    def step(weighted, xb):
        logits = jnp.dot(xb, cent.T, precision=lax.Precision.HIGHEST, preferred_element_type=jnp.float32) / tau
        top = lax.optimization_barrier(jnp.max(logits, axis=1))
        expo = jnp.exp(logits - top[:, None])
        total = lax.optimization_barrier(jnp.sum(expo, axis=1))
        resp = expo / total[:, None]
        weighted = weighted + jnp.dot(resp.T, xb, precision=lax.Precision.HIGHEST, preferred_element_type=jnp.float32)
        return (weighted, top + jnp.log(total))
    weighted, lognorm = lax.scan(step, jnp.zeros((K, D), jnp.float32), blocks)
    fresh = weighted / jnp.sqrt(lax.optimization_barrier(jnp.sum(weighted * weighted, axis=1, keepdims=True)) + 1e-06)
    return (fresh, lognorm.reshape(NPTS))

def reference(points, centroids):
    cent = centroids
    lognorm = jnp.zeros((NPTS,), jnp.float32)
    for turn in range(ITERS):
        cent, lognorm = one_iteration(points, cent)
    return (cent.reshape(N_CEN, K_DEV, D), lognorm)
```

```python
import jax
import jax.numpy as jnp
from jax import lax
from jax.sharding import Mesh, PartitionSpec as P

ITERS = 2
TAU = 0.1
SIZES = {"y": 4, "zh": 4, "x": 4, "zl": 4, "core": 2}
PT = ("y", "zh", "x")
CEN = ("zl", "core")


def dot(a, b, dims):
    return lax.dot_general(
        a,
        b,
        (dims, ((), ())),
        precision=lax.Precision.HIGH,
        preferred_element_type=jnp.float32,
    )


def group_size(axes):
    n = 1
    for axis in axes:
        n *= lax.axis_size(axis)
    return n


def gather(block, axes):
    n = group_size(axes)
    copies = jnp.broadcast_to(block[None], (n,) + block.shape)
    return lax.all_to_all(copies, axes, split_axis=0, concat_axis=0, tiled=True)


def scatter_sum(rows, axes):
    n = group_size(axes)
    blocks = rows.reshape(n, rows.shape[0] // n, rows.shape[1])
    return jnp.sum(lax.all_to_all(blocks, axes, split_axis=0, concat_axis=0, tiled=True), axis=0)


def renormalise(weighted):
    return weighted / jnp.sqrt(jnp.sum(weighted * weighted, axis=1, keepdims=True) + 1e-06)


def shards(points, centroids):
    current = centroids
    for turn in range(ITERS):
        logits = dot(points, current, ((1,), (1,))) / TAU
        local_top = jnp.max(logits, axis=1)
        expo = jnp.exp(logits - local_top[:, None])
        both = gather(jnp.stack([local_top, jnp.sum(expo, axis=1)]), CEN)
        tops, sums = both[:, 0], both[:, 1]
        top = jnp.max(tops, axis=0)
        total = jnp.sum(sums * jnp.exp(tops - top), axis=0)
        resp = expo * (jnp.exp(local_top - top) / total)[:, None]
        weighted = dot(resp, points, ((0,), (0,)))
        if turn < ITERS - 1:
            part = scatter_sum(weighted, ("y", "x"))
            mine = renormalise(jnp.sum(gather(part, ("zh",)), axis=0))
            current = gather(mine, ("y", "x")).reshape(centroids.shape)
    owned = renormalise(scatter_sum(scatter_sum(weighted, ("y",)), ("zh", "x")))
    return owned[None], top + jnp.log(total)


def solution(mesh):
    fine = Mesh(mesh.devices.reshape(tuple(SIZES.values())), tuple(SIZES))
    return jax.shard_map(
        shards,
        mesh=fine,
        in_specs=(P(PT, None), P(CEN, None)),
        out_specs=(P(CEN, PT, None), P(PT)),
        check_vma=False,
    )
```

```python
import jax
import jax.numpy as jnp
from jax import lax
from jax.sharding import Mesh, PartitionSpec as P

TAU = 0.1
SIZES = {"y": 4, "zh": 4, "x": 4, "zl": 4, "core": 2}
PT = ("y", "zh", "x")
CEN = ("zl", "core")


def dot(a, b, dims):
    return lax.dot_general(
        a,
        b,
        (dims, ((), ())),
        precision=lax.Precision.HIGH,
        preferred_element_type=jnp.float32,
    )


def group_size(axes):
    n = 1
    for axis in axes:
        n *= lax.axis_size(axis)
    return n


def gather(block, axes):
    n = group_size(axes)
    copies = jnp.broadcast_to(block[None], (n,) + block.shape)
    return lax.all_to_all(copies, axes, split_axis=0, concat_axis=0, tiled=True)


def scatter_sum(rows, axes):
    n = group_size(axes)
    blocks = rows.reshape(n, rows.shape[0] // n, rows.shape[1])
    return jnp.sum(lax.all_to_all(blocks, axes, split_axis=0, concat_axis=0, tiled=True), axis=0)


def renormalise(weighted):
    return weighted / jnp.sqrt(jnp.sum(weighted * weighted, axis=1, keepdims=True) + 1e-06)


def lse(values, axis):
    top = jnp.max(values, axis=axis, keepdims=True)
    expo = jnp.exp(values - top)
    return jnp.squeeze(top, axis), expo, jnp.squeeze(top, axis) + jnp.log(jnp.sum(expo, axis=axis))


def shards(points, centroids):
    half = points.shape[0] // 2
    core = lax.axis_index("core")
    share = lax.dynamic_slice_in_dim(points, core * half, half, 0)
    first = lax.all_gather(share, "y", axis=0, tiled=True)

    logits = dot(points, centroids, ((1,), (1,))) / TAU
    top, expo, local = lse(logits, 1)
    _, _, total = lse(gather(local, CEN), 0)
    resp = expo * jnp.exp(top - total)[:, None]
    weighted = dot(resp, points, ((0,), (0,)))
    part = scatter_sum(weighted, ("y", "x"))
    mine = renormalise(jnp.sum(gather(part, ("zh",)), axis=0))

    other = lax.ppermute(first, "core", [(0, 1), (1, 0)])
    current = gather(mine, ("x",)).reshape(-1, centroids.shape[1])
    parts = []
    for block in (first, other):
        top, expo, local = lse(dot(block, current, ((1,), (1,))) / TAU, 1)
        parts.append((top, expo, local))
    local = jnp.stack([parts[0][2], parts[1][2]])
    local = jnp.where(core == 0, local, local[::-1])
    _, _, total = lse(gather(local, ("y",) + CEN), 0)
    log_norm = lax.dynamic_slice_in_dim(total, lax.axis_index("y") * half, half, 1).reshape(-1)
    total = jnp.where(core == 0, total, total[::-1])
    weighted = 0.0
    for i, block in enumerate((first, other)):
        resp = parts[i][1] * jnp.exp(parts[i][0] - total[i])[:, None]
        weighted += dot(resp, block, ((0,), (0,)))
    owned = renormalise(scatter_sum(weighted, ("zh", "x")))
    return owned[None], log_norm


def solution(mesh):
    fine = Mesh(mesh.devices.reshape(tuple(SIZES.values())), tuple(SIZES))
    return jax.shard_map(
        shards,
        mesh=fine,
        in_specs=(P(PT, None), P(CEN, None)),
        out_specs=(P(CEN, PT, None), P(PT)),
        check_vma=False,
    )
```

```python
import jax
import jax.numpy as jnp
from jax import lax
from jax.sharding import Mesh, PartitionSpec as P

TAU = 0.1
SIZES = {"y": 4, "zh": 4, "x": 4, "zl": 4, "core": 2}
PT = ("y", "zh", "x")
CEN = ("zl", "core")


def dot(a, b, dims):
    return lax.dot_general(
        a,
        b,
        (dims, ((), ())),
        precision=lax.Precision.HIGH,
        preferred_element_type=jnp.float32,
    )


def group_size(axes):
    n = 1
    for axis in axes:
        n *= lax.axis_size(axis)
    return n


def gather(block, axes):
    n = group_size(axes)
    copies = jnp.broadcast_to(block[None], (n,) + block.shape)
    return lax.all_to_all(copies, axes, split_axis=0, concat_axis=0, tiled=True)


def scatter_sum(rows, axes):
    n = group_size(axes)
    blocks = rows.reshape(n, rows.shape[0] // n, rows.shape[1])
    return jnp.sum(lax.all_to_all(blocks, axes, split_axis=0, concat_axis=0, tiled=True), axis=0)


def renormalise(weighted):
    return weighted / jnp.sqrt(jnp.sum(weighted * weighted, axis=1, keepdims=True) + 1e-06)


def lse(values, axis):
    top = jnp.max(values, axis=axis, keepdims=True)
    expo = jnp.exp(values - top)
    return jnp.squeeze(top, axis), expo, jnp.squeeze(top, axis) + jnp.log(jnp.sum(expo, axis=axis))


def shards(points, centroids):
    half = points.shape[0] // 2
    core = lax.axis_index("core")
    share = lax.dynamic_slice_in_dim(points, core * half, half, 0)
    ring = lax.all_gather(share, "y", axis=0, tiled=True)

    logits = dot(points, centroids, ((1,), (1,))) / TAU
    top, expo, local = lse(logits, 1)
    _, _, total = lse(gather(local, CEN), 0)
    resp = expo * jnp.exp(top - total)[:, None]
    weighted = dot(resp, points, ((0,), (0,)))
    part = scatter_sum(weighted, ("y", "x"))
    mine = renormalise(jnp.sum(gather(part, ("zh",)), axis=0))

    current = gather(mine, ("core", "x")).reshape(-1, centroids.shape[1])
    top, expo, local = lse(dot(ring, current, ((1,), (1,))) / TAU, 1)
    _, _, total = lse(gather(local, ("y", "zl")), 0)
    here = lax.dynamic_slice_in_dim(total, lax.axis_index("y") * half, half, 0)
    there = lax.ppermute(here, "core", [(0, 1), (1, 0)])
    log_norm = jnp.where(core == 0, jnp.concatenate([here, there]), jnp.concatenate([there, here]))
    resp = expo * jnp.exp(top - total)[:, None]
    weighted = dot(resp, ring, ((0,), (0,)))
    owned = renormalise(scatter_sum(scatter_sum(weighted, ("core",)), ("zh", "x")))
    return owned[None], log_norm


def solution(mesh):
    fine = Mesh(mesh.devices.reshape(tuple(SIZES.values())), tuple(SIZES))
    return jax.shard_map(
        shards,
        mesh=fine,
        in_specs=(P(PT, None), P(CEN, None)),
        out_specs=(P(CEN, PT, None), P(PT)),
        check_vma=False,
    )
```

```python
import jax
import jax.numpy as jnp
from jax import lax
from jax.sharding import Mesh, PartitionSpec as P

ITERS = 2
TAU = 0.1
SIZES = {"y": 4, "zh": 4, "x": 4, "zl": 4, "core": 2}
PT = ("y", "zh", "x")
CEN = ("zl", "core")


def dot(a, b, dims):
    return lax.dot_general(
        a,
        b,
        (dims, ((), ())),
        precision=lax.Precision.HIGH,
        preferred_element_type=jnp.float32,
    )


def group_size(axes):
    n = 1
    for axis in axes:
        n *= lax.axis_size(axis)
    return n


def gather(block, axes):
    n = group_size(axes)
    copies = jnp.broadcast_to(block[None], (n,) + block.shape)
    return lax.all_to_all(copies, axes, split_axis=0, concat_axis=0, tiled=True)


def scatter_sum(rows, axes):
    n = group_size(axes)
    blocks = rows.reshape(n, rows.shape[0] // n, rows.shape[1])
    return jnp.sum(lax.all_to_all(blocks, axes, split_axis=0, concat_axis=0, tiled=True), axis=0)


def renormalise(weighted):
    return weighted / jnp.sqrt(jnp.sum(weighted * weighted, axis=1, keepdims=True) + 1e-06)


def lse(values, axis):
    top = jnp.max(values, axis=axis, keepdims=True)
    expo = jnp.exp(values - top)
    return jnp.squeeze(top, axis), expo, jnp.squeeze(top, axis) + jnp.log(jnp.sum(expo, axis=axis))


def shards(points, centroids):
    split = tuple(lax.axis_size(axis) for axis in PT)
    current = centroids.reshape(split + (-1, centroids.shape[1])).swapaxes(1, 2).reshape(centroids.shape)
    for turn in range(ITERS):
        logits = dot(points, current, ((1,), (1,))) / TAU
        top, expo, local = lse(logits, 1)
        _, _, total = lse(gather(local, CEN), 0)
        resp = expo * jnp.exp(top - total)[:, None]
        weighted = dot(resp, points, ((0,), (0,)))
        part = scatter_sum(weighted, ("y", "x"))
        if turn < ITERS - 1:
            mine = renormalise(jnp.sum(gather(part, ("zh",)), axis=0))
            current = gather(mine, ("y", "x")).reshape(centroids.shape)
    owned = renormalise(scatter_sum(part, ("zh",)))
    return owned[None], total


def solution(mesh):
    fine = Mesh(mesh.devices.reshape(tuple(SIZES.values())), tuple(SIZES))
    return jax.shard_map(
        shards,
        mesh=fine,
        in_specs=(P(PT, None), P(CEN, None)),
        out_specs=(P(CEN, PT, None), P(PT)),
        check_vma=False,
    )
```

```python
import jax
import jax.numpy as jnp
from jax import lax
from jax.experimental import pallas as pl
from jax.experimental.pallas import tpu as pltpu
from jax.sharding import Mesh, PartitionSpec as P

ITERS = 2
TAU = 0.1
SIZES = {"y": 4, "zh": 4, "x": 4, "zl": 4, "core": 2}
PT = ("y", "zh", "x")
CEN = ("zl", "core")
WIDTH = 256


def dot(a, b, dims):
    return lax.dot_general(
        a,
        b,
        (dims, ((), ())),
        precision=lax.Precision.HIGH,
        preferred_element_type=jnp.float32,
    )


def halves(x):
    high = x.astype(jnp.bfloat16)
    return high, (x - high.astype(jnp.float32)).astype(jnp.bfloat16)


def group_size(axes):
    n = 1
    for axis in axes:
        n *= lax.axis_size(axis)
    return n


def gather(block, axes):
    n = group_size(axes)
    copies = jnp.broadcast_to(block[None], (n,) + block.shape)
    return lax.all_to_all(copies, axes, split_axis=0, concat_axis=0, tiled=True)


def scatter_sum(rows, axes):
    n = group_size(axes)
    blocks = rows.reshape(n, rows.shape[0] // n, rows.shape[1])
    return jnp.sum(lax.all_to_all(blocks, axes, split_axis=0, concat_axis=0, tiled=True), axis=0)


def renormalise(weighted):
    return weighted / jnp.sqrt(jnp.sum(weighted * weighted, axis=1, keepdims=True) + 1e-06)


def lse(values, axis):
    top = jnp.max(values, axis=axis, keepdims=True)
    return top + jnp.log(jnp.sum(jnp.exp(values - top), axis=axis, keepdims=True))


def first_kernel(split, points, centroids, logits, local, xs, cs, ordered, chigh, clow, xsem, csem):
    ny, nz, nx, rows = split
    chunk = nz * nx * rows
    xcopies = [
        pltpu.make_async_copy(points.at[pl.ds(i * WIDTH, WIDTH)], xs.at[pl.ds(i * WIDTH, WIDTH)], xsem.at[i])
        for i in range(points.shape[0] // WIDTH)
    ]
    ccopies = [
        pltpu.make_async_copy(centroids.at[pl.ds(i * chunk, chunk)], cs.at[pl.ds(i * chunk, chunk)], csem.at[i])
        for i in range(ny)
    ]
    for copy in ccopies + xcopies:
        copy.start()
    for y in range(ny):
        ccopies[y].wait()
        for z in range(nz):
            for x in range(nx):
                here = y * chunk + (z * nx + x) * rows
                there = y * chunk + (x * nz + z) * rows
                ordered[there : there + rows, :] = cs[here : here + rows, :]
        part = slice(y * chunk, (y + 1) * chunk)
        chigh[part, :], clow[part, :] = halves(ordered[part, :])
    nt = (((1,), (1,)), ((), ()))
    for i, copy in enumerate(xcopies):
        copy.wait()
        part = slice(i * WIDTH, (i + 1) * WIDTH)
        high, low = halves(xs[part, :])
        value = lax.dot_general(chigh[...], high, nt, preferred_element_type=jnp.float32)
        value += lax.dot_general(chigh[...], low, nt, preferred_element_type=jnp.float32)
        value += lax.dot_general(clow[...], high, nt, preferred_element_type=jnp.float32)
        value = value / TAU
        logits[:, part] = value
        local[:, part] = lse(value, 0)


def first_logits(points, centroids, split):
    n, d = points.shape
    k = centroids.shape[0]
    return pl.pallas_call(
        lambda *refs: first_kernel(split, *refs),
        out_shape=(
            jax.ShapeDtypeStruct((k, n), jnp.float32),
            jax.ShapeDtypeStruct((1, n), jnp.float32),
        ),
        in_specs=[pl.BlockSpec(memory_space=pltpu.HBM)] * 2,
        out_specs=(pl.BlockSpec(memory_space=pltpu.VMEM),) * 2,
        scratch_shapes=[
            pltpu.VMEM((n, d), jnp.float32),
            pltpu.VMEM((k, d), jnp.float32),
            pltpu.VMEM((k, d), jnp.float32),
            pltpu.VMEM((k, d), jnp.bfloat16),
            pltpu.VMEM((k, d), jnp.bfloat16),
            pltpu.SemaphoreType.DMA((n // WIDTH,)),
            pltpu.SemaphoreType.DMA((split[0],)),
        ],
        compiler_params=pltpu.CompilerParams(vmem_limit_bytes=60 * 2**20),
    )(points, centroids)


def shards(points, centroids):
    split = tuple(lax.axis_size(axis) for axis in PT)
    split += (centroids.shape[0] // (split[0] * split[1] * split[2]),)
    logits, local = first_logits(points, centroids, split)
    for turn in range(ITERS):
        if turn:
            logits = dot(current, points, ((1,), (1,))) / TAU
            local = lse(logits, 0)
        total = lse(gather(local, CEN), 0)[0, 0]
        weighted = dot(jnp.exp(logits - total[None]), points, ((1,), (0,)))
        part = scatter_sum(weighted, ("y", "x"))
        if turn < ITERS - 1:
            mine = renormalise(jnp.sum(gather(part, ("zh",)), axis=0))
            current = gather(mine, ("y", "x")).reshape(centroids.shape)
    owned = renormalise(scatter_sum(part, ("zh",)))
    return owned[None], total


def solution(mesh):
    fine = Mesh(mesh.devices.reshape(tuple(SIZES.values())), tuple(SIZES))
    return jax.shard_map(
        shards,
        mesh=fine,
        in_specs=(P(PT, None), P(CEN, None)),
        out_specs=(P(CEN, PT, None), P(PT)),
        check_vma=False,
    )
```

```python
import jax
import jax.numpy as jnp
from jax import lax
from jax.experimental import pallas as pl
from jax.experimental.pallas import tpu as pltpu
from jax.sharding import Mesh, PartitionSpec as P

ITERS = 2
TAU = 0.1
SIZES = {"y": 4, "zh": 4, "x": 4, "zl": 4, "core": 2}
PT = ("y", "zh", "x")
CEN = ("zl", "core")


def dot(a, b, dims):
    return lax.dot_general(
        a,
        b,
        (dims, ((), ())),
        precision=lax.Precision.HIGH,
        preferred_element_type=jnp.float32,
    )


def halves(x):
    high = x.astype(jnp.bfloat16)
    return high, (x - high.astype(jnp.float32)).astype(jnp.bfloat16)


def group_size(axes):
    n = 1
    for axis in axes:
        n *= lax.axis_size(axis)
    return n


def gather(block, axes):
    n = group_size(axes)
    copies = jnp.broadcast_to(block[None], (n,) + block.shape)
    return lax.all_to_all(copies, axes, split_axis=0, concat_axis=0, tiled=True)


def scatter_sum(rows, axes):
    n = group_size(axes)
    blocks = rows.reshape(n, rows.shape[0] // n, rows.shape[1])
    return jnp.sum(lax.all_to_all(blocks, axes, split_axis=0, concat_axis=0, tiled=True), axis=0)


def renormalise(weighted):
    return weighted / jnp.sqrt(jnp.sum(weighted * weighted, axis=1, keepdims=True) + 1e-06)


def lse(values, axis):
    top = jnp.max(values, axis=axis, keepdims=True)
    return top + jnp.log(jnp.sum(jnp.exp(values - top), axis=axis, keepdims=True))


PIECES = 2


def first_kernel(split, points, centroids, logits, local, xs, cs, ordered, xsem, csem):
    ny, nz, nx, rows = split
    width = points.shape[1] // PIECES
    columns = [slice(i * width, (i + 1) * width) for i in range(PIECES)]
    ccopies = [pltpu.make_async_copy(centroids.at[:, c], cs.at[:, c], csem.at[i]) for i, c in enumerate(columns)]
    xcopies = [pltpu.make_async_copy(points.at[:, c], xs.at[:, c], xsem.at[i]) for i, c in enumerate(columns)]
    for ccopy, xcopy in zip(ccopies, xcopies):
        ccopy.start()
        xcopy.start()
    nt = (((1,), (1,)), ((), ()))
    total = None
    for i, c in enumerate(columns):
        ccopies[i].wait()
        for y in range(ny):
            for z in range(nz):
                for x in range(nx):
                    here = ((y * nz + z) * nx + x) * rows
                    there = ((y * nx + x) * nz + z) * rows
                    ordered[there : there + rows, c] = cs[here : here + rows, c]
        chigh, clow = halves(ordered[:, c])
        xcopies[i].wait()
        high, low = halves(xs[:, c])
        value = lax.dot_general(chigh, high, nt, preferred_element_type=jnp.float32)
        value += lax.dot_general(chigh, low, nt, preferred_element_type=jnp.float32)
        value += lax.dot_general(clow, high, nt, preferred_element_type=jnp.float32)
        if i:
            value += logits[...]
        if i == PIECES - 1:
            value = value / TAU
            local[...] = lse(value, 0)
        logits[...] = value


def first_logits(points, centroids, split):
    n, d = points.shape
    k = centroids.shape[0]
    return pl.pallas_call(
        lambda *refs: first_kernel(split, *refs),
        out_shape=(
            jax.ShapeDtypeStruct((k, n), jnp.float32),
            jax.ShapeDtypeStruct((1, n), jnp.float32),
        ),
        in_specs=[pl.BlockSpec(memory_space=pltpu.HBM)] * 2,
        out_specs=(pl.BlockSpec(memory_space=pltpu.VMEM),) * 2,
        scratch_shapes=[
            pltpu.VMEM((n, d), jnp.float32),
            pltpu.VMEM((k, d), jnp.float32),
            pltpu.VMEM((k, d), jnp.float32),
            pltpu.SemaphoreType.DMA((PIECES,)),
            pltpu.SemaphoreType.DMA((PIECES,)),
        ],
        compiler_params=pltpu.CompilerParams(vmem_limit_bytes=52 * 2**20 + 640 * 2**10),
    )(points, centroids)


def shards(points, centroids):
    split = tuple(lax.axis_size(axis) for axis in PT)
    split += (centroids.shape[0] // (split[0] * split[1] * split[2]),)
    logits, local = first_logits(points, centroids, split)
    for turn in range(ITERS):
        if turn:
            logits = dot(current, points, ((1,), (1,))) / TAU
            local = lse(logits, 0)
        total = lse(gather(local, CEN), 0)[0, 0]
        weighted = dot(jnp.exp(logits - total[None]), points, ((1,), (0,)))
        part = scatter_sum(weighted, ("y", "x"))
        if turn < ITERS - 1:
            mine = renormalise(jnp.sum(gather(part, ("zh",)), axis=0))
            current = gather(mine, ("y", "x")).reshape(centroids.shape)
    owned = renormalise(scatter_sum(part, ("zh",)))
    return owned[None], total


def solution(mesh):
    fine = Mesh(mesh.devices.reshape(tuple(SIZES.values())), tuple(SIZES))
    return jax.shard_map(
        shards,
        mesh=fine,
        in_specs=(P(PT, None), P(CEN, None)),
        out_specs=(P(CEN, PT, None), P(PT)),
        check_vma=False,
    )
```

```python
import jax
import jax.numpy as jnp
from jax import lax
from jax.experimental import pallas as pl
from jax.experimental.pallas import tpu as pltpu
from jax.sharding import Mesh, PartitionSpec as P

ITERS = 2
TAU = 0.1
SIZES = {"y": 4, "zh": 4, "x": 4, "zl": 4, "core": 2}
PT = ("y", "zh", "x")
CEN = ("zl", "core")


def dot(a, b, dims):
    return lax.dot_general(
        a,
        b,
        (dims, ((), ())),
        precision=lax.Precision.HIGH,
        preferred_element_type=jnp.float32,
    )


def halves(x):
    high = x.astype(jnp.bfloat16)
    return high, (x - high.astype(jnp.float32)).astype(jnp.bfloat16)


def group_size(axes):
    n = 1
    for axis in axes:
        n *= lax.axis_size(axis)
    return n


def gather(block, axes):
    n = group_size(axes)
    copies = jnp.broadcast_to(block[None], (n,) + block.shape)
    return lax.all_to_all(copies, axes, split_axis=0, concat_axis=0, tiled=True)


def scatter_sum(rows, axes):
    n = group_size(axes)
    blocks = rows.reshape(n, rows.shape[0] // n, rows.shape[1])
    return jnp.sum(lax.all_to_all(blocks, axes, split_axis=0, concat_axis=0, tiled=True), axis=0)


def ring_sum(part):
    for pairs in (((0, 1), (2, 3)), ((1, 2), (3, 0))):
        part += lax.ppermute(part, "zh", [p for a, b in pairs for p in ((a, b), (b, a))])
    return part


def renormalise(weighted):
    return weighted / jnp.sqrt(jnp.sum(weighted * weighted, axis=1, keepdims=True) + 1e-06)


def lse(values, axis):
    top = jnp.max(values, axis=axis, keepdims=True)
    return top + jnp.log(jnp.sum(jnp.exp(values - top), axis=axis, keepdims=True))


PIECES = 2


def first_kernel(split, points, centroids, logits, local, xs, cs, ordered, xsem, csem):
    ny, nz, nx, rows = split
    width = points.shape[1] // PIECES
    columns = [slice(i * width, (i + 1) * width) for i in range(PIECES)]
    ccopies = [pltpu.make_async_copy(centroids.at[:, c], cs.at[:, c], csem.at[i]) for i, c in enumerate(columns)]
    xcopies = [pltpu.make_async_copy(points.at[:, c], xs.at[:, c], xsem.at[i]) for i, c in enumerate(columns)]
    for ccopy, xcopy in zip(ccopies, xcopies):
        ccopy.start()
        xcopy.start()
    nt = (((1,), (1,)), ((), ()))
    total = None
    for i, c in enumerate(columns):
        ccopies[i].wait()
        for y in range(ny):
            for z in range(nz):
                for x in range(nx):
                    here = ((y * nz + z) * nx + x) * rows
                    there = ((y * nx + x) * nz + z) * rows
                    ordered[there : there + rows, c] = cs[here : here + rows, c]
        chigh, clow = halves(ordered[:, c])
        xcopies[i].wait()
        high, low = halves(xs[:, c])
        value = lax.dot_general(chigh, high, nt, preferred_element_type=jnp.float32)
        value += lax.dot_general(chigh, low, nt, preferred_element_type=jnp.float32)
        value += lax.dot_general(clow, high, nt, preferred_element_type=jnp.float32)
        if i:
            value += logits[...]
        if i == PIECES - 1:
            value = value / TAU
            local[...] = lse(value, 0)
        logits[...] = value


def first_logits(points, centroids, split):
    n, d = points.shape
    k = centroids.shape[0]
    return pl.pallas_call(
        lambda *refs: first_kernel(split, *refs),
        out_shape=(
            jax.ShapeDtypeStruct((k, n), jnp.float32),
            jax.ShapeDtypeStruct((1, n), jnp.float32),
        ),
        in_specs=[pl.BlockSpec(memory_space=pltpu.HBM)] * 2,
        out_specs=(pl.BlockSpec(memory_space=pltpu.VMEM),) * 2,
        scratch_shapes=[
            pltpu.VMEM((n, d), jnp.float32),
            pltpu.VMEM((k, d), jnp.float32),
            pltpu.VMEM((k, d), jnp.float32),
            pltpu.SemaphoreType.DMA((PIECES,)),
            pltpu.SemaphoreType.DMA((PIECES,)),
        ],
        compiler_params=pltpu.CompilerParams(vmem_limit_bytes=52 * 2**20 + 640 * 2**10),
    )(points, centroids)


def shards(points, centroids):
    split = tuple(lax.axis_size(axis) for axis in PT)
    split += (centroids.shape[0] // (split[0] * split[1] * split[2]),)
    logits, local = first_logits(points, centroids, split)
    for turn in range(ITERS):
        if turn:
            logits = dot(current, points, ((1,), (1,))) / TAU
            local = lse(logits, 0)
        total = lse(gather(local, CEN), 0)[0, 0]
        weighted = dot(jnp.exp(logits - total[None]), points, ((1,), (0,)))
        part = scatter_sum(weighted, ("y", "x"))
        if turn < ITERS - 1:
            mine = renormalise(ring_sum(part))
            current = gather(mine, ("y", "x")).reshape(centroids.shape)
    owned = renormalise(scatter_sum(part, ("zh",)))
    return owned[None], total


def solution(mesh):
    fine = Mesh(mesh.devices.reshape(tuple(SIZES.values())), tuple(SIZES))
    return jax.shard_map(
        shards,
        mesh=fine,
        in_specs=(P(PT, None), P(CEN, None)),
        out_specs=(P(CEN, PT, None), P(PT)),
        check_vma=False,
    )
```

```python
import jax
import jax.numpy as jnp
from jax import lax
from jax.experimental import pallas as pl
from jax.experimental.pallas import tpu as pltpu
from jax.sharding import Mesh, PartitionSpec as P

ITERS = 2
TAU = 0.1
SIZES = {"y": 4, "zh": 4, "x": 4, "zl": 4, "core": 2}
PT = ("y", "zh", "x")
CEN = ("zl", "core")


def dot(a, b, dims):
    return lax.dot_general(
        a,
        b,
        (dims, ((), ())),
        precision=lax.Precision.HIGH,
        preferred_element_type=jnp.float32,
    )


def halves(x):
    high = x.astype(jnp.bfloat16)
    return high, (x - high.astype(jnp.float32)).astype(jnp.bfloat16)


def group_size(axes):
    n = 1
    for axis in axes:
        n *= lax.axis_size(axis)
    return n


def gather(block, axes):
    n = group_size(axes)
    copies = jnp.broadcast_to(block[None], (n,) + block.shape)
    return lax.all_to_all(copies, axes, split_axis=0, concat_axis=0, tiled=True)


def scatter_sum(rows, axes):
    n = group_size(axes)
    blocks = rows.reshape(n, rows.shape[0] // n, rows.shape[1])
    return jnp.sum(lax.all_to_all(blocks, axes, split_axis=0, concat_axis=0, tiled=True), axis=0)


def renormalise(weighted):
    return weighted / jnp.sqrt(jnp.sum(weighted * weighted, axis=1, keepdims=True) + 1e-06)


def lse(values, axis):
    top = jnp.max(values, axis=axis, keepdims=True)
    return top + jnp.log(jnp.sum(jnp.exp(values - top), axis=axis, keepdims=True))


PIECES = 2


def first_kernel(split, points, centroids, logits, local, xs, cs, ordered, xsem, csem):
    ny, nz, nx, rows = split
    width = points.shape[1] // PIECES
    columns = [slice(i * width, (i + 1) * width) for i in range(PIECES)]
    ccopies = [pltpu.make_async_copy(centroids.at[:, c], cs.at[:, c], csem.at[i]) for i, c in enumerate(columns)]
    xcopies = [pltpu.make_async_copy(points.at[:, c], xs.at[:, c], xsem.at[i]) for i, c in enumerate(columns)]
    for ccopy, xcopy in zip(ccopies, xcopies):
        ccopy.start()
        xcopy.start()
    nt = (((1,), (1,)), ((), ()))
    total = None
    for i, c in enumerate(columns):
        ccopies[i].wait()
        for y in range(ny):
            for z in range(nz):
                for x in range(nx):
                    here = ((y * nz + z) * nx + x) * rows
                    there = ((y * nx + x) * nz + z) * rows
                    ordered[there : there + rows, c] = cs[here : here + rows, c]
        chigh, clow = halves(ordered[:, c])
        xcopies[i].wait()
        high, low = halves(xs[:, c])
        value = lax.dot_general(chigh, high, nt, preferred_element_type=jnp.float32)
        value += lax.dot_general(chigh, low, nt, preferred_element_type=jnp.float32)
        value += lax.dot_general(clow, high, nt, preferred_element_type=jnp.float32)
        if i:
            value += logits[...]
        if i == PIECES - 1:
            value = value / TAU
            local[...] = lse(value, 0)
        logits[...] = value


def first_logits(points, centroids, split):
    n, d = points.shape
    k = centroids.shape[0]
    return pl.pallas_call(
        lambda *refs: first_kernel(split, *refs),
        out_shape=(
            jax.ShapeDtypeStruct((k, n), jnp.float32),
            jax.ShapeDtypeStruct((1, n), jnp.float32),
        ),
        in_specs=[pl.BlockSpec(memory_space=pltpu.HBM)] * 2,
        out_specs=(pl.BlockSpec(memory_space=pltpu.VMEM),) * 2,
        scratch_shapes=[
            pltpu.VMEM((n, d), jnp.float32),
            pltpu.VMEM((k, d), jnp.float32),
            pltpu.VMEM((k, d), jnp.float32),
            pltpu.SemaphoreType.DMA((PIECES,)),
            pltpu.SemaphoreType.DMA((PIECES,)),
        ],
        compiler_params=pltpu.CompilerParams(vmem_limit_bytes=52 * 2**20 + 640 * 2**10),
    )(points, centroids)


def shards(points, centroids):
    split = tuple(lax.axis_size(axis) for axis in PT)
    split += (centroids.shape[0] // (split[0] * split[1] * split[2]),)
    logits, local = first_logits(points, centroids, split)
    for turn in range(ITERS):
        if turn:
            logits = dot(current, points, ((1,), (1,))) / TAU
            local = lse(logits, 0)
        total = lse(gather(local, CEN), 0)[0, 0]
        weighted = dot(jnp.exp(logits - total[None]), points, ((1,), (0,)))
        part = scatter_sum(weighted, ("y", "x"))
        if turn < ITERS - 1:
            mine = renormalise(jnp.sum(lax.all_gather(part, "zh"), axis=0))
            current = gather(mine, ("y", "x")).reshape(centroids.shape)
    owned = renormalise(scatter_sum(part, ("zh",)))
    return owned[None], total


def solution(mesh):
    fine = Mesh(mesh.devices.reshape(tuple(SIZES.values())), tuple(SIZES))
    return jax.shard_map(
        shards,
        mesh=fine,
        in_specs=(P(PT, None), P(CEN, None)),
        out_specs=(P(CEN, PT, None), P(PT)),
        check_vma=False,
    )
```

```python
import itertools

import jax
import jax.numpy as jnp
from jax import lax
from jax.experimental import pallas as pl
from jax.experimental.pallas import tpu as pltpu
from jax.sharding import Mesh, PartitionSpec as P

ITERS = 2
TAU = 0.1
SIZES = {"y": 4, "zh": 4, "x": 4, "zl": 4, "core": 2}
PT = ("y", "zh", "x")
CEN = ("zl", "core")
PLANE = ("y", "x", "core")


def dot(a, b, dims):
    return lax.dot_general(
        a,
        b,
        (dims, ((), ())),
        precision=lax.Precision.HIGH,
        preferred_element_type=jnp.float32,
    )


def halves(x):
    high = x.astype(jnp.bfloat16)
    return high, (x - high.astype(jnp.float32)).astype(jnp.bfloat16)


def group_size(axes):
    n = 1
    for axis in axes:
        n *= lax.axis_size(axis)
    return n


def plane_groups():
    ny, nx, nc = (lax.axis_size(axis) for axis in PLANE)
    first = [(y * nx + x) * nc for y in range(ny) for x in range(nx)]
    second = [(y * nx + x) * nc + 1 for x in range(nx) for y in range(ny)]
    return [first, second]


def swap(blocks, axes):
    groups = plane_groups() if axes == PLANE else None
    return lax.all_to_all(blocks, axes, split_axis=0, concat_axis=0, tiled=True, axis_index_groups=groups)


def count(axes):
    return group_size(axes[:2] if axes == PLANE else axes)


def gather(block, axes):
    return swap(jnp.broadcast_to(block[None], (count(axes),) + block.shape), axes)


def scatter_sum(rows, axes):
    n = count(axes)
    return jnp.sum(swap(rows.reshape(n, rows.shape[0] // n, rows.shape[1]), axes), axis=0)


def renormalise(weighted):
    return weighted / jnp.sqrt(jnp.sum(weighted * weighted, axis=1, keepdims=True) + 1e-06)


def lse(values, axis):
    top = jnp.max(values, axis=axis, keepdims=True)
    return top + jnp.log(jnp.sum(jnp.exp(values - top), axis=axis, keepdims=True))


PIECES = 2


def first_kernel(split, points, centroids, logits, local, xs, cs, ordered, xsem, csem):
    ny, nz, nx, rows = split
    core = lax.axis_index("core")
    width = points.shape[1] // PIECES
    columns = [slice(i * width, (i + 1) * width) for i in range(PIECES)]
    ccopies = [pltpu.make_async_copy(centroids.at[:, c], cs.at[:, c], csem.at[i]) for i, c in enumerate(columns)]
    xcopies = [pltpu.make_async_copy(points.at[:, c], xs.at[:, c], xsem.at[i]) for i, c in enumerate(columns)]
    for ccopy, xcopy in zip(ccopies, xcopies):
        ccopy.start()
        xcopy.start()
    nt = (((1,), (1,)), ((), ()))
    total = None
    for i, c in enumerate(columns):
        ccopies[i].wait()
        for number in range(2):

            @pl.when(core == number)
            def _():
                for y, z, x in itertools.product(range(ny), range(nz), range(nx)):
                    here = ((y * nz + z) * nx + x) * rows
                    block = x * ny + y if number else y * nx + x
                    there = (block * nz + z) * rows
                    ordered[there : there + rows, c] = cs[here : here + rows, c]

        chigh, clow = halves(ordered[:, c])
        xcopies[i].wait()
        high, low = halves(xs[:, c])
        value = lax.dot_general(chigh, high, nt, preferred_element_type=jnp.float32)
        value += lax.dot_general(chigh, low, nt, preferred_element_type=jnp.float32)
        value += lax.dot_general(clow, high, nt, preferred_element_type=jnp.float32)
        if i:
            value += logits[...]
        if i == PIECES - 1:
            value = value / TAU
            local[...] = lse(value, 0)
        logits[...] = value


def first_logits(points, centroids, split):
    n, d = points.shape
    k = centroids.shape[0]
    return pl.pallas_call(
        lambda *refs: first_kernel(split, *refs),
        out_shape=(
            jax.ShapeDtypeStruct((k, n), jnp.float32),
            jax.ShapeDtypeStruct((1, n), jnp.float32),
        ),
        in_specs=[pl.BlockSpec(memory_space=pltpu.HBM)] * 2,
        out_specs=(pl.BlockSpec(memory_space=pltpu.VMEM),) * 2,
        scratch_shapes=[
            pltpu.VMEM((n, d), jnp.float32),
            pltpu.VMEM((k, d), jnp.float32),
            pltpu.VMEM((k, d), jnp.float32),
            pltpu.SemaphoreType.DMA((PIECES,)),
            pltpu.SemaphoreType.DMA((PIECES,)),
        ],
        compiler_params=pltpu.CompilerParams(vmem_limit_bytes=52 * 2**20 + 640 * 2**10),
    )(points, centroids)


def shards(points, centroids):
    split = tuple(lax.axis_size(axis) for axis in PT)
    split += (centroids.shape[0] // (split[0] * split[1] * split[2]),)
    logits, local = first_logits(points, centroids, split)
    for turn in range(ITERS):
        if turn:
            logits = dot(current, points, ((1,), (1,))) / TAU
            local = lse(logits, 0)
        total = lse(gather(local, CEN), 0)[0, 0]
        weighted = dot(jnp.exp(logits - total[None]), points, ((1,), (0,)))
        part = scatter_sum(weighted, PLANE)
        if turn < ITERS - 1:
            mine = renormalise(jnp.sum(lax.all_gather(part, "zh"), axis=0))
            current = gather(mine, PLANE).reshape(centroids.shape)
    owned = renormalise(scatter_sum(part, ("zh",)))
    return owned[None], total


def solution(mesh):
    fine = Mesh(mesh.devices.reshape(tuple(SIZES.values())), tuple(SIZES))
    return jax.shard_map(
        shards,
        mesh=fine,
        in_specs=(P(PT, None), P(CEN, None)),
        out_specs=(P(CEN, PT, None), P(PT)),
        check_vma=False,
    )
```

```python
import jax
import jax.numpy as jnp
from jax import lax
from jax.experimental import pallas as pl
from jax.experimental.pallas import tpu as pltpu
from jax.sharding import Mesh, PartitionSpec as P

ITERS = 2
TAU = 0.1
SIZES = {"y": 4, "zh": 4, "x": 4, "zl": 4, "core": 2}
PT = ("y", "zh", "x")
CEN = ("zl", "core")


def dot(a, b, dims):
    return lax.dot_general(
        a,
        b,
        (dims, ((), ())),
        precision=lax.Precision.HIGH,
        preferred_element_type=jnp.float32,
    )


def halves(x):
    high = x.astype(jnp.bfloat16)
    return high, (x - high.astype(jnp.float32)).astype(jnp.bfloat16)


def group_size(axes):
    n = 1
    for axis in axes:
        n *= lax.axis_size(axis)
    return n


def gather(block, axes):
    n = group_size(axes)
    copies = jnp.broadcast_to(block[None], (n,) + block.shape)
    return lax.all_to_all(copies, axes, split_axis=0, concat_axis=0, tiled=True)


def scatter_sum(rows, axes):
    n = group_size(axes)
    blocks = rows.reshape(n, rows.shape[0] // n, rows.shape[1])
    return jnp.sum(lax.all_to_all(blocks, axes, split_axis=0, concat_axis=0, tiled=True), axis=0)


def exchange(keep, send, pairs):
    return keep + lax.ppermute(send, "zh", [p for a, b in pairs for p in ((a, b), (b, a))])


def ring_scatter(rows):
    z = lax.axis_index("zh")
    for upper, pairs in (((0, 3), ((0, 1), (2, 3))), ((0, 1), ((1, 2), (3, 0)))):
        top, low = jnp.split(rows, 2)
        up = (z == upper[0]) | (z == upper[1])
        rows = exchange(jnp.where(up, top, low), jnp.where(up, low, top), pairs)
    return rows


def renormalise(weighted):
    return weighted / jnp.sqrt(jnp.sum(weighted * weighted, axis=1, keepdims=True) + 1e-06)


def lse(values, axis):
    top = jnp.max(values, axis=axis, keepdims=True)
    return top + jnp.log(jnp.sum(jnp.exp(values - top), axis=axis, keepdims=True))


PIECES = 2
RING = (0, 3, 1, 2)


def first_kernel(split, points, centroids, logits, local, xs, cs, ordered, xsem, csem):
    ny, nz, nx, rows = split
    width = points.shape[1] // PIECES
    columns = [slice(i * width, (i + 1) * width) for i in range(PIECES)]
    ccopies = [pltpu.make_async_copy(centroids.at[:, c], cs.at[:, c], csem.at[i]) for i, c in enumerate(columns)]
    xcopies = [pltpu.make_async_copy(points.at[:, c], xs.at[:, c], xsem.at[i]) for i, c in enumerate(columns)]
    for ccopy, xcopy in zip(ccopies, xcopies):
        ccopy.start()
        xcopy.start()
    nt = (((1,), (1,)), ((), ()))
    total = None
    for i, c in enumerate(columns):
        ccopies[i].wait()
        for y in range(ny):
            for z in range(nz):
                for x in range(nx):
                    here = ((y * nz + z) * nx + x) * rows
                    there = ((y * nx + x) * nz + RING.index(z)) * rows
                    ordered[there : there + rows, c] = cs[here : here + rows, c]
        chigh, clow = halves(ordered[:, c])
        xcopies[i].wait()
        high, low = halves(xs[:, c])
        value = lax.dot_general(chigh, high, nt, preferred_element_type=jnp.float32)
        value += lax.dot_general(chigh, low, nt, preferred_element_type=jnp.float32)
        value += lax.dot_general(clow, high, nt, preferred_element_type=jnp.float32)
        if i:
            value += logits[...]
        if i == PIECES - 1:
            value = value / TAU
            local[...] = lse(value, 0)
        logits[...] = value


def first_logits(points, centroids, split):
    n, d = points.shape
    k = centroids.shape[0]
    return pl.pallas_call(
        lambda *refs: first_kernel(split, *refs),
        out_shape=(
            jax.ShapeDtypeStruct((k, n), jnp.float32),
            jax.ShapeDtypeStruct((1, n), jnp.float32),
        ),
        in_specs=[pl.BlockSpec(memory_space=pltpu.HBM)] * 2,
        out_specs=(pl.BlockSpec(memory_space=pltpu.VMEM),) * 2,
        scratch_shapes=[
            pltpu.VMEM((n, d), jnp.float32),
            pltpu.VMEM((k, d), jnp.float32),
            pltpu.VMEM((k, d), jnp.float32),
            pltpu.SemaphoreType.DMA((PIECES,)),
            pltpu.SemaphoreType.DMA((PIECES,)),
        ],
        compiler_params=pltpu.CompilerParams(vmem_limit_bytes=52 * 2**20 + 640 * 2**10),
    )(points, centroids)


def shards(points, centroids):
    split = tuple(lax.axis_size(axis) for axis in PT)
    split += (centroids.shape[0] // (split[0] * split[1] * split[2]),)
    logits, local = first_logits(points, centroids, split)
    for turn in range(ITERS):
        if turn:
            logits = dot(current, points, ((1,), (1,))) / TAU
            local = lse(logits, 0)
        total = lse(gather(local, CEN), 0)[0, 0]
        weighted = dot(jnp.exp(logits - total[None]), points, ((1,), (0,)))
        part = scatter_sum(weighted, ("y", "x"))
        if turn < ITERS - 1:
            mine = renormalise(jnp.sum(lax.all_gather(part, "zh"), axis=0))
            current = gather(mine, ("y", "x")).reshape(centroids.shape)
    owned = renormalise(ring_scatter(part))
    return owned[None], total


def solution(mesh):
    fine = Mesh(mesh.devices.reshape(tuple(SIZES.values())), tuple(SIZES))
    return jax.shard_map(
        shards,
        mesh=fine,
        in_specs=(P(PT, None), P(CEN, None)),
        out_specs=(P(CEN, PT, None), P(PT)),
        check_vma=False,
    )
```

```python
import itertools

import jax
import jax.numpy as jnp
from jax import lax
from jax.experimental import pallas as pl
from jax.experimental.pallas import tpu as pltpu
from jax.sharding import Mesh, PartitionSpec as P

ITERS = 2
TAU = 0.1
SIZES = {"y": 4, "zh": 4, "x": 4, "zl": 4, "core": 2}
PT = ("y", "zh", "x")
CEN = ("zl", "core")
PLANE = ("y", "x", "core")


def dot(a, b, dims):
    return lax.dot_general(
        a,
        b,
        (dims, ((), ())),
        precision=lax.Precision.HIGH,
        preferred_element_type=jnp.float32,
    )


def halves(x):
    high = x.astype(jnp.bfloat16)
    return high, (x - high.astype(jnp.float32)).astype(jnp.bfloat16)


def group_size(axes):
    n = 1
    for axis in axes:
        n *= lax.axis_size(axis)
    return n


def plane_groups():
    ny, nx, nc = (lax.axis_size(axis) for axis in PLANE)
    first = [(y * nx + x) * nc for y in range(ny) for x in range(nx)]
    second = [(y * nx + x) * nc + 1 for x in range(nx) for y in range(ny)]
    return [first, second]


def swap(blocks, axes):
    groups = plane_groups() if axes == PLANE else None
    return lax.all_to_all(blocks, axes, split_axis=0, concat_axis=0, tiled=True, axis_index_groups=groups)


def count(axes):
    return group_size(axes[:2] if axes == PLANE else axes)


def gather(block, axes):
    return swap(jnp.broadcast_to(block[None], (count(axes),) + block.shape), axes)


def scatter_sum(rows, axes):
    n = count(axes)
    return jnp.sum(swap(rows.reshape(n, rows.shape[0] // n, rows.shape[1]), axes), axis=0)


def renormalise(weighted):
    return weighted / jnp.sqrt(jnp.sum(weighted * weighted, axis=1, keepdims=True) + 1e-06)


def lse(values, axis):
    top = jnp.max(values, axis=axis, keepdims=True)
    return top + jnp.log(jnp.sum(jnp.exp(values - top), axis=axis, keepdims=True))


PIECES = 2


def first_kernel(split, points, centroids, logits, local, xs, cs, ordered, xsem, csem):
    ny, nz, nx, rows = split
    core = lax.axis_index("core")
    width = points.shape[1] // PIECES
    columns = [slice(i * width, (i + 1) * width) for i in range(PIECES)]
    ccopies = [pltpu.make_async_copy(centroids.at[:, c], cs.at[:, c], csem.at[i]) for i, c in enumerate(columns)]
    xcopies = [pltpu.make_async_copy(points.at[:, c], xs.at[:, c], xsem.at[i]) for i, c in enumerate(columns)]
    for ccopy, xcopy in zip(ccopies, xcopies):
        ccopy.start()
        xcopy.start()
    nt = (((1,), (1,)), ((), ()))
    total = None
    for i, c in enumerate(columns):
        ccopies[i].wait()
        for number in range(2):

            @pl.when(core == number)
            def _():
                for y, z, x in itertools.product(range(ny), range(nz), range(nx)):
                    here = ((y * nz + z) * nx + x) * rows
                    block = x * ny + y if number else y * nx + x
                    there = (block * nz + z) * rows
                    ordered[there : there + rows, c] = cs[here : here + rows, c]

        chigh, clow = halves(ordered[:, c])
        xcopies[i].wait()
        high, low = halves(xs[:, c])
        value = lax.dot_general(chigh, high, nt, preferred_element_type=jnp.float32)
        value += lax.dot_general(chigh, low, nt, preferred_element_type=jnp.float32)
        value += lax.dot_general(clow, high, nt, preferred_element_type=jnp.float32)
        if i:
            value += logits[...]
        if i == PIECES - 1:
            value = value / TAU
            local[...] = lse(value, 0)
        logits[...] = value


def first_logits(points, centroids, split):
    n, d = points.shape
    k = centroids.shape[0]
    return pl.pallas_call(
        lambda *refs: first_kernel(split, *refs),
        out_shape=(
            jax.ShapeDtypeStruct((k, n), jnp.float32),
            jax.ShapeDtypeStruct((1, n), jnp.float32),
        ),
        in_specs=[pl.BlockSpec(memory_space=pltpu.HBM)] * 2,
        out_specs=(pl.BlockSpec(memory_space=pltpu.VMEM),) * 2,
        scratch_shapes=[
            pltpu.VMEM((n, d), jnp.float32),
            pltpu.VMEM((k, d), jnp.float32),
            pltpu.VMEM((k, d), jnp.float32),
            pltpu.SemaphoreType.DMA((PIECES,)),
            pltpu.SemaphoreType.DMA((PIECES,)),
        ],
        compiler_params=pltpu.CompilerParams(vmem_limit_bytes=52 * 2**20 + 640 * 2**10),
    )(points, centroids)


def shards(points, centroids):
    split = tuple(lax.axis_size(axis) for axis in PT)
    split += (centroids.shape[0] // (split[0] * split[1] * split[2]),)
    logits, local = first_logits(points, centroids, split)
    for turn in range(ITERS):
        if turn:
            logits = dot(current, points, ((1,), (1,))) / TAU
            local = lse(logits, 0)
        total = lse(gather(local, CEN), 0)[0, 0]
        weighted = dot(jnp.exp(logits - total[None]), points, ((1,), (0,)))
        part = scatter_sum(weighted, PLANE)
        if turn < ITERS - 1:
            mine = renormalise(jnp.sum(lax.all_gather(part, "zh"), axis=0))
            current = gather(mine, PLANE).reshape(centroids.shape)
    rows = part.shape[0] // lax.axis_size("zh")
    blocks = lax.dynamic_slice_in_dim(lax.all_gather(part, "zh"), lax.axis_index("zh") * rows, rows, 1)
    owned = renormalise(jnp.sum(blocks, axis=0))
    return owned[None], total


def solution(mesh):
    fine = Mesh(mesh.devices.reshape(tuple(SIZES.values())), tuple(SIZES))
    return jax.shard_map(
        shards,
        mesh=fine,
        in_specs=(P(PT, None), P(CEN, None)),
        out_specs=(P(CEN, PT, None), P(PT)),
        check_vma=False,
    )
```

```python
import itertools

import jax
import jax.numpy as jnp
from jax import lax
from jax.experimental import pallas as pl
from jax.experimental.pallas import tpu as pltpu
from jax.sharding import Mesh, PartitionSpec as P

ITERS = 2
TAU = 0.1
SIZES = {"y": 4, "zh": 4, "x": 4, "zl": 4, "core": 2}
PT = ("y", "zh", "x")
CEN = ("zl", "core")
PLANE = ("y", "x", "core")


def dot(a, b, dims):
    return lax.dot_general(
        a,
        b,
        (dims, ((), ())),
        precision=lax.Precision.HIGH,
        preferred_element_type=jnp.float32,
    )


def halves(x):
    high = x.astype(jnp.bfloat16)
    return high, (x - high.astype(jnp.float32)).astype(jnp.bfloat16)


def group_size(axes):
    n = 1
    for axis in axes:
        n *= lax.axis_size(axis)
    return n


def plane_groups():
    ny, nx, nc = (lax.axis_size(axis) for axis in PLANE)
    first = [(y * nx + x) * nc for y in range(ny) for x in range(nx)]
    second = [(y * nx + x) * nc + 1 for x in range(nx) for y in range(ny)]
    return [first, second]


def swap(blocks, axes):
    groups = plane_groups() if axes == PLANE else None
    return lax.all_to_all(blocks, axes, split_axis=0, concat_axis=0, tiled=True, axis_index_groups=groups)


def count(axes):
    return group_size(axes[:2] if axes == PLANE else axes)


def gather(block, axes):
    return swap(jnp.broadcast_to(block[None], (count(axes),) + block.shape), axes)


def scatter_sum(rows, axes):
    n = count(axes)
    return jnp.sum(swap(rows.reshape(n, rows.shape[0] // n, rows.shape[1]), axes), axis=0)


def renormalise(weighted):
    return weighted / jnp.sqrt(jnp.sum(weighted * weighted, axis=1, keepdims=True) + 1e-06)


def lse(values, axis):
    top = jnp.max(values, axis=axis, keepdims=True)
    return top + jnp.log(jnp.sum(jnp.exp(values - top), axis=axis, keepdims=True))


PIECES = 2


def first_kernel(split, points, centroids, logits, local, xs, cs, ordered, xsem, csem):
    ny, nz, nx, rows = split
    core = lax.axis_index("core")
    width = points.shape[1] // PIECES
    columns = [slice(i * width, (i + 1) * width) for i in range(PIECES)]
    ccopies = [pltpu.make_async_copy(centroids.at[:, c], cs.at[:, c], csem.at[i]) for i, c in enumerate(columns)]
    xcopies = [pltpu.make_async_copy(points.at[:, c], xs.at[:, c], xsem.at[i]) for i, c in enumerate(columns)]
    for ccopy, xcopy in zip(ccopies, xcopies):
        ccopy.start()
        xcopy.start()
    nt = (((1,), (1,)), ((), ()))
    total = None
    for i, c in enumerate(columns):
        ccopies[i].wait()
        for number in range(2):

            @pl.when(core == number)
            def _():
                for y, z, x in itertools.product(range(ny), range(nz), range(nx)):
                    here = ((y * nz + z) * nx + x) * rows
                    block = x * ny + y if number else y * nx + x
                    there = (block * nz + z) * rows
                    ordered[there : there + rows, c] = cs[here : here + rows, c]

        chigh, clow = halves(ordered[:, c])
        xcopies[i].wait()
        high, low = halves(xs[:, c])
        value = lax.dot_general(chigh, high, nt, preferred_element_type=jnp.float32)
        value += lax.dot_general(chigh, low, nt, preferred_element_type=jnp.float32)
        value += lax.dot_general(clow, high, nt, preferred_element_type=jnp.float32)
        if i:
            value += logits[...]
        if i == PIECES - 1:
            value = value / TAU
            local[...] = lse(value, 0)
        logits[...] = value


def first_logits(points, centroids, split):
    n, d = points.shape
    k = centroids.shape[0]
    return pl.pallas_call(
        lambda *refs: first_kernel(split, *refs),
        out_shape=(
            jax.ShapeDtypeStruct((k, n), jnp.float32),
            jax.ShapeDtypeStruct((1, n), jnp.float32),
        ),
        in_specs=[pl.BlockSpec(memory_space=pltpu.HBM)] * 2,
        out_specs=(pl.BlockSpec(memory_space=pltpu.VMEM),) * 2,
        scratch_shapes=[
            pltpu.VMEM((n, d), jnp.float32),
            pltpu.VMEM((k, d), jnp.float32),
            pltpu.VMEM((k, d), jnp.float32),
            pltpu.SemaphoreType.DMA((PIECES,)),
            pltpu.SemaphoreType.DMA((PIECES,)),
        ],
        compiler_params=pltpu.CompilerParams(vmem_limit_bytes=52 * 2**20 + 640 * 2**10),
    )(points, centroids)


def shards(points, centroids):
    split = tuple(lax.axis_size(axis) for axis in PT)
    split += (centroids.shape[0] // (split[0] * split[1] * split[2]),)
    logits, local = first_logits(points, centroids, split)
    for turn in range(ITERS):
        if turn:
            logits = dot(current, points, ((1,), (1,)))
            local = lse(logits, 0)
        total = lse(gather(local, CEN), 0)[0, 0]
        weighted = dot(jnp.exp(logits - total[None]), points, ((1,), (0,)))
        part = scatter_sum(weighted, PLANE)
        if turn < ITERS - 1:
            mine = renormalise(jnp.sum(lax.all_gather(part, "zh"), axis=0))
            current = gather(mine / TAU, PLANE).reshape(centroids.shape)
    owned = renormalise(scatter_sum(part, ("zh",)))
    return owned[None], total


def solution(mesh):
    fine = Mesh(mesh.devices.reshape(tuple(SIZES.values())), tuple(SIZES))
    return jax.shard_map(
        shards,
        mesh=fine,
        in_specs=(P(PT, None), P(CEN, None)),
        out_specs=(P(CEN, PT, None), P(PT)),
        check_vma=False,
    )
```

```python
import itertools

import jax
import jax.numpy as jnp
from jax import lax
from jax.experimental import pallas as pl
from jax.experimental.pallas import tpu as pltpu
from jax.sharding import Mesh, PartitionSpec as P

ITERS = 2
TAU = 0.1
SIZES = {"y": 4, "zh": 4, "x": 4, "zl": 4, "core": 2}
PT = ("y", "zh", "x")
CEN = ("zl", "core")
PLANE = ("y", "x", "core")


def dot(a, b, dims):
    return lax.dot_general(
        a,
        b,
        (dims, ((), ())),
        precision=lax.Precision.HIGH,
        preferred_element_type=jnp.float32,
    )


def halves(x):
    high = x.astype(jnp.bfloat16)
    return high, (x - high.astype(jnp.float32)).astype(jnp.bfloat16)


def group_size(axes):
    n = 1
    for axis in axes:
        n *= lax.axis_size(axis)
    return n


def plane_groups():
    ny, nx, nc = (lax.axis_size(axis) for axis in PLANE)
    first = [(y * nx + x) * nc for y in range(ny) for x in range(nx)]
    second = [(y * nx + x) * nc + 1 for x in range(nx) for y in range(ny)]
    return [first, second]


def swap(blocks, axes):
    groups = plane_groups() if axes == PLANE else None
    return lax.all_to_all(blocks, axes, split_axis=0, concat_axis=0, tiled=True, axis_index_groups=groups)


def count(axes):
    return group_size(axes[:2] if axes == PLANE else axes)


def gather(block, axes):
    return swap(jnp.broadcast_to(block[None], (count(axes),) + block.shape), axes)


def scatter_sum(rows, axes):
    n = count(axes)
    return jnp.sum(swap(rows.reshape(n, rows.shape[0] // n, rows.shape[1]), axes), axis=0)


def renormalise(weighted):
    return weighted / jnp.sqrt(jnp.sum(weighted * weighted, axis=1, keepdims=True) + 1e-06)


def lse(values, axis):
    top = jnp.max(values, axis=axis, keepdims=True)
    return top + jnp.log(jnp.sum(jnp.exp(values - top), axis=axis, keepdims=True))


PIECES = 2


def first_kernel(split, points, centroids, logits, local, xs, cs, ordered, xsem, csem):
    ny, nz, nx, rows = split
    core = lax.axis_index("core")
    width = points.shape[1] // PIECES
    columns = [slice(i * width, (i + 1) * width) for i in range(PIECES)]
    ccopies = [pltpu.make_async_copy(centroids.at[:, c], cs.at[:, c], csem.at[i]) for i, c in enumerate(columns)]
    xcopies = [pltpu.make_async_copy(points.at[:, c], xs.at[:, c], xsem.at[i]) for i, c in enumerate(columns)]
    for ccopy, xcopy in zip(ccopies, xcopies):
        ccopy.start()
        xcopy.start()
    nt = (((1,), (1,)), ((), ()))
    total = None
    for i, c in enumerate(columns):
        ccopies[i].wait()
        for number in range(2):

            @pl.when(core == number)
            def _():
                for y, z, x in itertools.product(range(ny), range(nz), range(nx)):
                    here = ((y * nz + z) * nx + x) * rows
                    block = x * ny + y if number else y * nx + x
                    there = (block * nz + z) * rows
                    ordered[there : there + rows, c] = cs[here : here + rows, c]

        chigh, clow = halves(ordered[:, c])
        xcopies[i].wait()
        high, low = halves(xs[:, c])
        value = lax.dot_general(chigh, high, nt, preferred_element_type=jnp.float32)
        value += lax.dot_general(chigh, low, nt, preferred_element_type=jnp.float32)
        value += lax.dot_general(clow, high, nt, preferred_element_type=jnp.float32)
        if i:
            value += logits[...]
        if i == PIECES - 1:
            value = value / TAU
            local[...] = lse(value, 0)
        logits[...] = value


def first_logits(points, centroids, split):
    n, d = points.shape
    k = centroids.shape[0]
    return pl.pallas_call(
        lambda *refs: first_kernel(split, *refs),
        out_shape=(
            jax.ShapeDtypeStruct((k, n), jnp.float32),
            jax.ShapeDtypeStruct((1, n), jnp.float32),
        ),
        in_specs=[pl.BlockSpec(memory_space=pltpu.HBM)] * 2,
        out_specs=(pl.BlockSpec(memory_space=pltpu.VMEM),) * 2,
        scratch_shapes=[
            pltpu.VMEM((n, d), jnp.float32),
            pltpu.VMEM((k, d), jnp.float32),
            pltpu.VMEM((k, d), jnp.float32),
            pltpu.SemaphoreType.DMA((PIECES,)),
            pltpu.SemaphoreType.DMA((PIECES,)),
        ],
        compiler_params=pltpu.CompilerParams(vmem_limit_bytes=52 * 2**20 + 640 * 2**10),
    )(points, centroids)


def shards(points, centroids):
    split = tuple(lax.axis_size(axis) for axis in PT)
    split += (centroids.shape[0] // (split[0] * split[1] * split[2]),)
    logits, local = first_logits(points, centroids, split)
    for turn in range(ITERS):
        if turn:
            logits = dot(current, points, ((1,), (1,))) / TAU
            local = lse(logits, 0)
        total = lse(gather(local, CEN[::-1]), 0)[0, 0]
        weighted = dot(jnp.exp(logits - total[None]), points, ((1,), (0,)))
        part = scatter_sum(weighted, PLANE)
        if turn < ITERS - 1:
            mine = renormalise(jnp.sum(lax.all_gather(part, "zh"), axis=0))
            current = gather(mine, PLANE).reshape(centroids.shape)
    owned = renormalise(scatter_sum(part, ("zh",)))
    return owned[None], total


def solution(mesh):
    fine = Mesh(mesh.devices.reshape(tuple(SIZES.values())), tuple(SIZES))
    return jax.shard_map(
        shards,
        mesh=fine,
        in_specs=(P(PT, None), P(CEN, None)),
        out_specs=(P(CEN, PT, None), P(PT)),
        check_vma=False,
    )
```
